256 devices in a mesh: gx: 8 (over y_lo, x), gz: 4 (over y_hi, core), ta: 8 (over z).
Axes of the slice: x: 4, y: 4 (y_hi: 2, y_lo: 2; y = y_hi * 2 + y_lo), z: 8, core: 2. Of those that a mesh axis runs over, the one named last changes fastest.
Arguments:
- velocity: bfloat16 [3, 64, 256, 4096], P(None, 'ta', 'gx', 'gz'), may hold values from -6 to 6
- offsets: int32 [7], replicated, may hold values from 0 to 48, as said below
- owner: int32 [7], replicated, may hold values from 0 to 31, as said below
Outputs:
- cross_spectra: float32 [4, 2, 7, 256, 4096], P(None, None, None, 'gx', ('gz', 'ta'))
The draws below stay inside these ranges and needn't reach their ends.
Inputs may be any that keep to these rules, and one draw needn't show every extreme that they name: `offsets`: each segment of 16 snapshots lies inside the window. owner o names the block of streamwise index o // 4 and spanwise index o mod 4.
All inputs are finite; a program needn't handle non-finite values.
Results may differ from the reference program's by a relative error of at most 0.0062.
Values may be sent and summed in bfloat16 or wider, within the bound.
A program may use at most 64 MiB of HBM per device.

```python
import math
import jax
import jax.numpy as jnp
from jax import lax

CX = 32
CZ = 1024
SEG = 16
NSEG = 7
F = 7
NT = 64
NX = 256
NZ = 4096
BLOCKS_X = 8
BLOCKS_Z = 4


def draw_offsets(key, part):
    latest = NT - SEG
    sampled_values = jax.random.randint(key, (NSEG,), 0, latest + 1)
    placing = jax.random.permutation(jax.random.fold_in(key, 7), NSEG)
    sampled_values = sampled_values.at[placing[0]].set(0)
    sampled_values = sampled_values.at[placing[1]].set(latest)
    return sampled_values.astype(jnp.int32)


def draw_owner(key, part):
    latest = BLOCKS_X * BLOCKS_Z - 1
    sampled_values = jax.random.randint(key, (NSEG,), 0, latest + 1)
    placing = jax.random.permutation(jax.random.fold_in(key, 11), NSEG)
    sampled_values = sampled_values.at[placing[0]].set(0)
    sampled_values = sampled_values.at[placing[1]].set(latest)
    return sampled_values.astype(jnp.int32)


def block_scale(rng, extent, split, smallest, high):
    level = 1.0
    for dim, blocks in split:
        steps = jax.random.uniform(jax.random.fold_in(jax.random.fold_in(rng, 6), dim), (blocks,), jnp.float32, smallest / len(split), high / len(split))
        level = level * jnp.repeat(jnp.exp(steps), extent[dim] // blocks).reshape((-1,) + (1,) * (len(extent) - 1 - dim))
    return level


def centred(stream_key, dims, scale, most, cuts=(), held_as=jnp.bfloat16):
    result = scale * jax.random.normal(stream_key, dims, jnp.float32)
    if cuts:
        result = result * block_scale(stream_key, dims, cuts, -0.22, 0.18)
    return jnp.clip(result, -most, most).astype(held_as)


def setup_inputs(seed: int = 0) -> dict:
    key_of = jax.random.split(jax.random.key(seed), 4)
    velocity = centred(key_of[0], (3, NT, NX, NZ), 1.0, 6.0, ((1, 8), (2, 8), (3, 4)))
    offsets = draw_offsets(jax.random.fold_in(key_of[3], 71), 0)
    owner = draw_owner(jax.random.fold_in(key_of[3], 71), 0)
    return {"velocity": velocity, "offsets": offsets, "owner": owner}


def wrapped_gradient(field, which_axis):
    ahead_one = jnp.roll(field, -1, which_axis)
    behind_one = jnp.roll(field, 1, which_axis)
    ahead_two = jnp.roll(field, -2, which_axis)
    behind_two = jnp.roll(field, 2, which_axis)
    return (8.0 * (ahead_one - behind_one) - (ahead_two - behind_two)) / 12.0


def dft_table(offsets, step_count_total):
    sample_times = jnp.arange(step_count_total, dtype=jnp.int32)
    temporal_delay = sample_times[None, :] - offsets[:, None].astype(jnp.int32)
    inside = (temporal_delay >= 0) & (temporal_delay < SEG)
    window = 0.5 - 0.5 * jnp.cos((2.0 * math.pi / SEG) * temporal_delay.astype(jnp.float32))
    frequency = jnp.arange(1, F + 1, dtype=jnp.int32)
    turns = (frequency[None, :, None] * temporal_delay[:, None, :]) % SEG
    phase_angle = (2.0 * math.pi / SEG) * turns.astype(jnp.float32)
    weight = jnp.where(inside, window, jnp.float32(0.0))[:, None, :]
    rows = jnp.stack([weight * jnp.cos(phase_angle), -weight * jnp.sin(phase_angle)], axis=1)
    return rows.reshape(offsets.shape[0] * 2 * F, step_count_total).astype(jnp.bfloat16)


def reference(velocity, offsets, owner):
    streamwise = velocity[0].astype(jnp.float32)
    spanwise = velocity[2].astype(jnp.float32)
    vorticity = (wrapped_gradient(streamwise, 2) - wrapped_gradient(spanwise, 1)).astype(jnp.bfloat16)
    fields = jnp.concatenate([velocity, vorticity[None]], axis=0)
    flat_fields = fields.reshape(4, NT, NX * NZ)
    window_rows = dft_table(jnp.zeros((1,), jnp.int32), SEG)
    zero_index = jnp.zeros((), jnp.int32)
    cospectrum = jnp.zeros((4, F, NX, NZ), jnp.float32)
    quadrature_spectrum = jnp.zeros((4, F, NX, NZ), jnp.float32)
    for segment in range(NSEG):
        window_piece = lax.dynamic_slice_in_dim(flat_fields, offsets[segment].astype(jnp.int32), SEG, 1)
        spectrum = jnp.stack([jnp.dot(window_rows, window_piece[quantity], preferred_element_type=jnp.float32) for quantity in range(4)])
        spectrum = spectrum.reshape(4, 2, F, NX, NZ)
        start_x = (owner[segment] // BLOCKS_Z).astype(jnp.int32) * CX
        start_z = (owner[segment] % BLOCKS_Z).astype(jnp.int32) * CZ
        block_data = lax.dynamic_slice(spectrum, (zero_index, zero_index, zero_index, start_x, start_z), (4, 2, F, CX, CZ))
        remote = jnp.tile(block_data, (1, 1, 1, BLOCKS_X, BLOCKS_Z))
        cospectrum = cospectrum + (remote[:, 0] * spectrum[:, 0] + remote[:, 1] * spectrum[:, 1])
        quadrature_spectrum = quadrature_spectrum + (remote[:, 0] * spectrum[:, 1] - remote[:, 1] * spectrum[:, 0])
    scaling = 8.0 / (3.0 * SEG * NSEG)
    return jnp.stack([cospectrum, quadrature_spectrum], axis=1) * scaling
```

```python
import math

import jax
import jax.numpy as jnp
import numpy as np
from jax import lax
from jax.experimental import pallas as pl
from jax.experimental.pallas import tpu as pltpu
from jax.sharding import PartitionSpec as P

SEG = 16
NSEG = 7
F = 7
J = NSEG * 2 * F
TILES = 100
PIECE = 25
PART = 7
MESH = pl.DeviceIdType.MESH
U, V, W, OM = 0, 1, 2, 3
BF = jnp.bfloat16
F32 = jnp.float32


def table_rows():
    lag = np.arange(SEG)
    window = 0.5 - 0.5 * np.cos(2.0 * math.pi / SEG * lag)
    turns = np.arange(1, F + 1)[:, None] * lag[None, :] % SEG
    phase = 2.0 * math.pi / SEG * turns
    rows = np.concatenate([window * np.cos(phase), -window * np.sin(phase)], axis=0)
    rows = rows.astype(np.float32).astype(jnp.bfloat16)
    return np.repeat(rows, 16, axis=0)


def slope(delta):
    out = np.zeros(delta.shape, np.float32)
    for shift, coefficient in ((1, 8.0), (-1, -8.0), (2, -1.0), (-2, 1.0)):
        out[delta == shift] = coefficient
    return out


def slope_tables():
    lane = np.arange(128)
    along_z = slope(lane[:, None] - lane[None, :])
    edge = np.array([-2, -1, 128, 129])
    edge_rows = slope(edge[:, None] - lane[None, :])
    halo_z = np.zeros((2, 16, 128), np.float32)
    halo_z[0, 0:4] = edge_rows
    halo_z[1, 4:8] = edge_rows
    snap_out = np.repeat(np.arange(8), 32)
    row_out = np.tile(np.arange(32), 8)
    snap_half = np.repeat(np.arange(8), 16)
    row_half = np.tile(np.arange(16), 8)
    snap_in = np.concatenate([snap_out, snap_half, snap_half])
    row_in = np.concatenate([row_out, row_half - 16, row_half + 32])
    along_x = slope(row_in[None, :] - row_out[:, None])
    along_x = along_x * (snap_in[None, :] == snap_out[:, None])
    cast = lambda a: a.astype(jnp.bfloat16)
    return cast(along_z), cast(halo_z), cast(along_x)


def kernel(
    vel, offsets, owner, rows_ref, dz_ref, bz_ref, dx_ref, out,
    recv, uext, hz_out, hz_in, h_lo, h_hi, om, wm, xs, spec,
    a_buf, c_0, c_1, c_2, c_3, d_buf, e_0, e_1, e_2, e_3, f_buf, g_0, g_1, g_2, g_3, p_buf, t_buf, out_v,
    own_core, own_1, own_2,
    a2a_s, a2a_r, hz_s, hz_r, edge_s, edge_r, halo_s, halo_r,
    core_s, core_r, l1_s, l1_r, l2_s, l2_r, g2_s, g2_r, g1_s, g1_r, gc_s, gc_r,
    loc_s, out_s,
):
    c_buf, e_buf, g_buf = (c_0, c_1, c_2, c_3), (e_0, e_1, e_2, e_3), (g_0, g_1, g_2, g_3)
    gx, gz, ta = lax.axis_index("gx"), lax.axis_index("gz"), lax.axis_index("ta")
    core = gz % 2
    x = gx % 4
    y = (gz // 2) * 2 + gx // 4

    def chip(px, py, pc):
        return ((py % 2) * 4 + px, (py // 2) * 2 + pc, ta)

    m1 = (1 - core) * x + core * y
    m2 = (1 - core) * y + core * x

    def peer_1(step):
        p = (m1 + step) % 4
        return p, chip((1 - core) * p + core * x, (1 - core) * y + core * p, core)

    def peer_2(step):
        p = (m2 + step) % 4
        return p, chip((1 - core) * x + core * p, (1 - core) * p + core * y, core)

    partner = (gx, (gz // 2) * 2 + 1 - core, ta)
    gx_up, gx_down = ((gx + 1) % 8, gz, ta), ((gx + 7) % 8, gz, ta)
    gz_up, gz_down = (gx, (gz + 1) % 4, ta), (gx, (gz + 3) % 4, ta)

    def remote(src, dst, send, recv_sem, device):
        return pltpu.make_async_remote_copy(
            src_ref=src, dst_ref=dst, send_sem=send, recv_sem=recv_sem,
            device_id=device, device_id_type=MESH,
        )

    everyone = [(gx, gz, (ta + d) % 8) for d in range(1, 8)]
    everyone += [peer_1(d)[1] for d in (1, 2, 3)] + [peer_2(d)[1] for d in (1, 2, 3)]
    everyone += [partner, gx_up, gx_down, gz_up, gz_down]
    barrier = pltpu.get_barrier_semaphore()
    for device in everyone:
        pl.semaphore_signal(barrier, inc=1, device_id=device, device_id_type=MESH)
    pl.semaphore_wait(barrier, len(everyone))

    order = (4, 3, 5, 2, 6, 1, 7)

    def columns(j):
        return pl.ds(pl.multiple_of(j * 128, 128), 128)

    def spread(field, slot):
        copies = []
        for n, d in enumerate(order):
            j = (ta + d) % 8
            copies.append(
                remote(
                    vel.at[field, :, :, columns(j)], recv.at[field, ta],
                    a2a_s.at[slot, n], a2a_r.at[slot, n], (gx, gz, j),
                )
            )
        for copy in copies:
            copy.start()
        mine = pltpu.make_async_copy(
            vel.at[field, :, :, columns(ta)], recv.at[field, ta], loc_s.at[slot]
        )
        mine.start()
        return copies, mine

    edge_up = remote(
        vel.at[U, :, :, 896:1024], uext.at[:, :, 0:128], edge_s.at[0], edge_r.at[0], gz_up
    )
    edge_down = remote(
        vel.at[U, :, :, 0:128], uext.at[:, :, 1152:1280], edge_s.at[1], edge_r.at[1], gz_down
    )
    edge_up.start()
    edge_down.start()
    body = pltpu.make_async_copy(vel.at[U], uext.at[:, :, 128:1152], loc_s.at[3])
    body.start()
    sent_w = spread(W, 0)
    sent_u = spread(U, 1)

    for s in range(NSEG):
        o = owner[s]
        o_gx, o_gz = o // 4, o % 4
        o_x, o_y = o_gx % 4, (o_gz // 2) * 2 + o_gx // 4
        own_core[s] = o_gz % 2
        own_1[s] = (1 - core) * o_x + core * o_y
        own_2[s] = (1 - core) * o_y + core * o_x

    body.wait()
    edge_up.wait_recv()
    edge_down.wait_recv()
    r_io = lax.broadcasted_iota(jnp.int32, (128, 1280), 0)
    l_io = lax.broadcasted_iota(jnp.int32, (128, 1280), 1)
    r16 = r_io % 16
    r4 = r16 % 4
    target = 128 + 128 * (r_io // 16) + r4 + jnp.where(r4 < 2, -2, 126)
    hit = l_io == target
    packed = jnp.zeros((128, 128), F32)
    for h in range(2):
        select = jnp.where(hit & (r16 // 4 == h), 1.0, 0.0).astype(BF)
        data = uext[4 * h : 4 * h + 4].reshape(128, 1280)
        packed += lax.dot_general(
            select, data, (((1,), (1,)), ((), ())), preferred_element_type=F32
        )
    hz_out[...] = packed.astype(BF).reshape(8, 16, 128)
    sent_hz = []
    for n, d in enumerate(order):
        j = (ta + d) % 8
        sent_hz.append(
            remote(hz_out.at[j], hz_in.at[ta], hz_s.at[n], hz_r.at[n], (gx, gz, j))
        )
    for copy in sent_hz:
        copy.start()
    hz_in[ta] = hz_out[ta]
    sent_v = spread(V, 2)

    col = lax.broadcasted_iota(jnp.int32, (16, 1024), 1)
    lag_io = lax.broadcasted_iota(jnp.int32, (16, 1024), 0)
    same = (
        lax.broadcasted_iota(jnp.int32, (224, 1024), 0) % 16
        == lax.broadcasted_iota(jnp.int32, (224, 1024), 1) % 16
    )

    def build(s, carry):
        one = jnp.where(col // 16 - offsets[s] == lag_io, 1.0, 0.0).astype(BF)
        full = jnp.dot(rows_ref[...], one, preferred_element_type=F32)
        wm[s] = jnp.where(same, full, 0.0).astype(BF)
        return carry

    lax.fori_loop(0, NSEG, build, 0)

    def transform(q, src):
        xs[:, 0:128] = src[:, :, 0:16, :].reshape(1024, 128)
        xs[:, 128:256] = src[:, :, 16:32, :].reshape(1024, 128)

        def one_segment(s, carry):
            r = jnp.dot(wm[s], xs[...], preferred_element_type=F32)
            rows = pl.ds(s * 14, 14)
            spec[q, rows] = r.reshape(14, 16, 256)
            lo = r[:, 0:128].astype(BF).reshape(14, 16, 128)
            hi = r[:, 128:256].astype(BF).reshape(14, 16, 128)
            c_buf[q][core, rows] = jnp.where(core == 0, lo, hi)
            a_buf[q, rows] = jnp.where(core == 0, hi, lo)
            return carry

        lax.fori_loop(0, NSEG, one_segment, 0)
        zero = jnp.zeros((2, 16, 128), BF)
        c_buf[q][core, J:TILES] = zero
        a_buf[q, J:TILES] = zero
        copy = remote(a_buf.at[q], c_buf[q].at[core], core_s.at[q], core_r.at[q], partner)
        copy.start()
        return [copy]

    def level_1(q, before):
        for copy in before:
            copy.wait_recv()
        for s in range(NSEG):
            d_buf[q, s * 14 : s * 14 + 14] = c_buf[q][own_core[s], s * 14 : s * 14 + 14]
        d_buf[q, J:TILES] = jnp.zeros((2, 16, 128), BF)
        copies = []
        for d in (2, 1, 3):
            p, device = peer_1(d)
            copies.append(
                remote(
                    d_buf.at[q, pl.ds(p * PIECE, PIECE)], e_buf[q].at[m1],
                    l1_s.at[q, d - 1], l1_r.at[q, d - 1], device,
                )
            )
        for copy in copies:
            copy.start()
        e_buf[q][m1] = d_buf[q, pl.ds(m1 * PIECE, PIECE)]
        return copies

    def level_2(q, before):
        for copy in before:
            copy.wait_recv()

        def pick(i, carry):
            i25 = jnp.minimum(i, PIECE - 1)
            s = jnp.minimum((m1 * PIECE + i25) // 14, NSEG - 1)
            f_buf[q, i] = e_buf[q][own_1[s], i25]
            return carry

        lax.fori_loop(0, 4 * PART, pick, 0)
        copies = []
        for d in (2, 1, 3):
            p, device = peer_2(d)
            copies.append(
                remote(
                    f_buf.at[q, pl.ds(p * PART, PART)], g_buf[q].at[m2],
                    l2_s.at[q, d - 1], l2_r.at[q, d - 1], device,
                )
            )
        for copy in copies:
            copy.start()
        g_buf[q][m2] = f_buf[q, pl.ds(m2 * PART, PART)]
        return copies

    def gather_2(q, before):
        for copy in before:
            copy.wait_recv()

        def pick(i, carry):
            i25 = jnp.minimum(m2 * PART + i, PIECE - 1)
            s = jnp.minimum((m1 * PIECE + i25) // 14, NSEG - 1)
            p_buf[q, m2 * PART + i] = g_buf[q][own_2[s], i]
            return carry

        lax.fori_loop(0, PART, pick, 0)
        part = p_buf.at[q, pl.ds(m2 * PART, PART)]
        copies = []
        for d in (2, 1, 3):
            copies.append(
                remote(part, part, g2_s.at[q, d - 1], g2_r.at[q, d - 1], peer_2(d)[1])
            )
        for copy in copies:
            copy.start()
        return copies

    def gather_1(q, before):
        for copy in before:
            copy.wait_recv()
        piece = t_buf.at[q, core, pl.ds(m1 * PIECE, PIECE)]
        copies = []
        for d in (2, 1, 3):
            copies.append(
                remote(
                    p_buf.at[q, 0:PIECE], piece,
                    g1_s.at[q, d - 1], g1_r.at[q, d - 1], peer_1(d)[1],
                )
            )
        for copy in copies:
            copy.start()
        t_buf[q, core, pl.ds(m1 * PIECE, PIECE)] = p_buf[q, 0:PIECE]
        return copies

    def gather_core(q, before):
        for copy in before:
            copy.wait_recv()
        half = t_buf.at[q, core]
        copy = remote(half, half, gc_s.at[q], gc_r.at[q], partner)
        copy.start()
        return [copy]

    scaling = 8.0 / (3.0 * SEG * NSEG)

    def finish(q, before):
        for copy in before:
            copy.wait_recv()

        def one_frequency(k, carry):
            for h in range(2):
                co = jnp.zeros((16, 128), F32)
                quad = jnp.zeros((16, 128), F32)
                for s in range(NSEG):
                    rc = t_buf[q, h, s * 14 + k].astype(F32)
                    rs = t_buf[q, h, s * 14 + F + k].astype(F32)
                    lc = spec[q, s * 14 + k, :, h * 128 : h * 128 + 128]
                    ls = spec[q, s * 14 + F + k, :, h * 128 : h * 128 + 128]
                    co += rc * lc + rs * ls
                    quad += rc * ls - rs * lc
                out_v[q, 0, k, h * 16 : h * 16 + 16, :] = co * scaling
                out_v[q, 1, k, h * 16 : h * 16 + 16, :] = quad * scaling
            return carry

        lax.fori_loop(0, F, one_frequency, 0)
        copy = pltpu.make_async_copy(out_v.at[q], out.at[q], out_s.at[q])
        copy.start()
        return copy

    started = []

    def run(step, q, before):
        copies = step(q, before)
        started.extend(copies)
        return copies

    def arrived(sent):
        copies, mine = sent
        mine.wait()
        for copy in copies:
            copy.wait_recv()

    arrived(sent_w)
    halo_up = remote(recv.at[W, :, :, 16:32], h_lo, halo_s.at[0], halo_r.at[0], gx_up)
    halo_down = remote(recv.at[W, :, :, 0:16], h_hi, halo_s.at[1], halo_r.at[1], gx_down)
    c_w = run(transform, W, recv.at[W])
    halo_up.start()
    halo_down.start()
    for step in (level_1, level_2, gather_2, gather_1, gather_core):
        c_w = run(step, W, c_w)
    arrived(sent_u)
    c_u = run(transform, U, recv.at[U])
    c_u = run(level_1, U, c_u)
    for copy in sent_hz:
        copy.wait_recv()
    halo_up.wait_recv()
    halo_down.wait_recv()

    def vorticity(i, carry):
        u_i = recv[U, i].reshape(256, 128)
        w_i = jnp.concatenate(
            [recv[W, i].reshape(256, 128), h_lo[i].reshape(128, 128), h_hi[i].reshape(128, 128)],
            axis=0,
        )
        across = jnp.dot(dx_ref[...], w_i, preferred_element_type=F32)
        inner = jnp.dot(u_i, dz_ref[...], preferred_element_type=F32)
        outer = jnp.concatenate(
            [
                lax.dot_general(
                    hz_in[i], bz_ref[h], (((0,), (0,)), ((), ())), preferred_element_type=F32
                )
                for h in range(2)
            ],
            axis=0,
        )
        om[i] = ((inner + outer - across) / 12.0).astype(BF).reshape(8, 32, 128)
        return carry

    lax.fori_loop(0, 8, vorticity, 0)
    c_o = run(transform, OM, om)
    c_u = run(level_2, U, c_u)
    c_o = run(level_1, OM, c_o)
    c_u = run(gather_2, U, c_u)
    c_o = run(level_2, OM, c_o)
    c_u = run(gather_1, U, c_u)
    c_o = run(gather_2, OM, c_o)
    outs = [finish(W, c_w)]
    c_u = run(gather_core, U, c_u)
    c_o = run(gather_1, OM, c_o)
    arrived(sent_v)
    c_v = run(transform, V, recv.at[V])
    c_o = run(gather_core, OM, c_o)
    c_v = run(level_1, V, c_v)
    outs.append(finish(U, c_u))
    c_v = run(level_2, V, c_v)
    c_v = run(gather_2, V, c_v)
    c_v = run(gather_1, V, c_v)
    outs.append(finish(OM, c_o))
    c_v = run(gather_core, V, c_v)
    outs.append(finish(V, c_v))

    for copies, _ in (sent_w, sent_u, sent_v):
        for copy in copies:
            copy.wait_send()
    for copy in sent_hz + started + [edge_up, edge_down, halo_up, halo_down]:
        copy.wait_send()
    for copy in outs:
        copy.wait()


def shards(velocity, offsets, owner):
    along_z, halo_z, along_x = slope_tables()
    dma = pltpu.SemaphoreType.DMA
    vmem = lambda *shape: pltpu.VMEM(shape, BF)
    scratch = [
        vmem(3, 8, 8, 32, 128), vmem(8, 32, 1280), vmem(8, 16, 128), vmem(8, 16, 128),
        vmem(8, 8, 16, 128), vmem(8, 8, 16, 128), vmem(8, 8, 32, 128),
        vmem(NSEG, 224, 1024), vmem(1024, 256), pltpu.VMEM((4, J, 16, 256), F32),
        vmem(4, TILES, 16, 128), *[vmem(2, TILES, 16, 128)] * 4, vmem(4, TILES, 16, 128),
        *[vmem(4, PIECE, 16, 128)] * 4, vmem(4, 4 * PART, 16, 128), *[vmem(4, PART, 16, 128)] * 4,
        vmem(4, 4 * PART, 16, 128), vmem(4, 2, TILES, 16, 128),
        pltpu.VMEM((4, 2, F, 32, 128), F32),
        pltpu.SMEM((NSEG,), jnp.int32), pltpu.SMEM((NSEG,), jnp.int32), pltpu.SMEM((NSEG,), jnp.int32),
        dma((3, 7)), dma((3, 7)), dma((7,)), dma((7,)), dma((2,)), dma((2,)), dma((2,)), dma((2,)),
        dma((4,)), dma((4,)), dma((4, 3)), dma((4, 3)), dma((4, 3)), dma((4, 3)),
        dma((4, 3)), dma((4, 3)), dma((4, 3)), dma((4, 3)), dma((4,)), dma((4,)),
        dma((4,)), dma((4,)),
    ]
    return pl.pallas_call(
        kernel,
        out_shape=jax.ShapeDtypeStruct((4, 2, F, 32, 128), F32),
        in_specs=[
            pl.BlockSpec(memory_space=pl.ANY),
            pl.BlockSpec(memory_space=pltpu.SMEM),
            pl.BlockSpec(memory_space=pltpu.SMEM),
        ]
        + [pl.BlockSpec(memory_space=pltpu.VMEM)] * 4,
        out_specs=pl.BlockSpec(memory_space=pl.ANY),
        scratch_shapes=scratch,
        compiler_params=pltpu.CompilerParams(
            collective_id=0, has_side_effects=True, vmem_limit_bytes=56 << 20
        ),
        name="cross_spectra",
    )(
        velocity, offsets, owner, jnp.asarray(table_rows()), jnp.asarray(along_z),
        jnp.asarray(halo_z), jnp.asarray(along_x),
    )


def solution(mesh):
    in_specs = (P(None, "ta", "gx", "gz"), P(), P())
    out_specs = P(None, None, None, "gx", ("gz", "ta"))
    return jax.shard_map(shards, mesh=mesh, in_specs=in_specs, out_specs=out_specs, check_vma=False)
```

```python
import math

import jax
import jax.numpy as jnp
import numpy as np
from jax import lax
from jax.experimental import pallas as pl
from jax.experimental.pallas import tpu as pltpu
from jax.sharding import PartitionSpec as P

SEG = 16
NSEG = 7
F = 7
J = NSEG * 2 * F
TILES = 100
PIECE = 25
MESH = pl.DeviceIdType.MESH
U, V, W, OM = 0, 1, 2, 3
BF = jnp.bfloat16
F32 = jnp.float32


def table_rows():
    lag = np.arange(SEG)
    window = 0.5 - 0.5 * np.cos(2.0 * math.pi / SEG * lag)
    turns = np.arange(1, F + 1)[:, None] * lag[None, :] % SEG
    phase = 2.0 * math.pi / SEG * turns
    rows = np.concatenate([window * np.cos(phase), -window * np.sin(phase)], axis=0)
    rows = rows.astype(np.float32).astype(jnp.bfloat16)
    return np.repeat(rows, 16, axis=0)


def slope(delta):
    out = np.zeros(delta.shape, np.float32)
    for shift, coefficient in ((1, 8.0), (-1, -8.0), (2, -1.0), (-2, 1.0)):
        out[delta == shift] = coefficient
    return out


def slope_tables():
    lane = np.arange(128)
    along_z = slope(lane[:, None] - lane[None, :])
    edge = np.array([-2, -1, 128, 129])
    edge_rows = slope(edge[:, None] - lane[None, :])
    halo_z = np.zeros((2, 16, 128), np.float32)
    halo_z[0, 0:4] = edge_rows
    halo_z[1, 4:8] = edge_rows
    snap_out = np.repeat(np.arange(8), 32)
    row_out = np.tile(np.arange(32), 8)
    snap_half = np.repeat(np.arange(8), 16)
    row_half = np.tile(np.arange(16), 8)
    snap_in = np.concatenate([snap_out, snap_half, snap_half])
    row_in = np.concatenate([row_out, row_half - 16, row_half + 32])
    along_x = slope(row_in[None, :] - row_out[:, None])
    along_x = along_x * (snap_in[None, :] == snap_out[:, None])
    cast = lambda a: a.astype(jnp.bfloat16)
    return cast(along_z), cast(halo_z), cast(along_x)


def kernel(
    vel, offsets, owner, rows_ref, dz_ref, bz_ref, dx_ref, out,
    recv, uext, hz_out, hz_in, h_lo, h_hi, om, wm, xs, spec,
    a_buf, c_0, c_1, c_2, c_3, d_buf, e_0, e_1, e_2, e_3, f_buf, g_0, g_1, g_2, g_3, t_buf, out_v,
    own_core, own_1, own_2, tile_1, tile_2,
    a2a_s, a2a_r, hz_s, hz_r, edge_s, edge_r, halo_s, halo_r,
    core_s, core_r, l1_s, l1_r, l2_s, l2_r, g1_s, g1_r, gc_s, gc_r,
    loc_s, out_s,
):
    c_buf, e_buf, g_buf = (c_0, c_1, c_2, c_3), (e_0, e_1, e_2, e_3), (g_0, g_1, g_2, g_3)
    gx, gz, ta = lax.axis_index("gx"), lax.axis_index("gz"), lax.axis_index("ta")
    core = gz % 2
    x = gx % 4
    y = (gz // 2) * 2 + gx // 4

    def chip(px, py, pc):
        return ((py % 2) * 4 + px, (py // 2) * 2 + pc, ta)

    m1 = (1 - core) * x + core * y
    m2 = (1 - core) * y + core * x

    def peer_1(step):
        p = (m1 + step) % 4
        return p, chip((1 - core) * p + core * x, (1 - core) * y + core * p, core)

    def peer_2(step):
        p = (m2 + step) % 4
        return p, chip((1 - core) * x + core * p, (1 - core) * p + core * y, core)

    partner = (gx, (gz // 2) * 2 + 1 - core, ta)
    gx_up, gx_down = ((gx + 1) % 8, gz, ta), ((gx + 7) % 8, gz, ta)
    gz_up, gz_down = (gx, (gz + 1) % 4, ta), (gx, (gz + 3) % 4, ta)

    def remote(src, dst, send, recv_sem, device):
        return pltpu.make_async_remote_copy(
            src_ref=src, dst_ref=dst, send_sem=send, recv_sem=recv_sem,
            device_id=device, device_id_type=MESH,
        )

    everyone = [(gx, gz, (ta + d) % 8) for d in range(1, 8)]
    everyone += [peer_1(d)[1] for d in (1, 2, 3)] + [peer_2(d)[1] for d in (1, 2, 3)]
    everyone += [partner, gx_up, gx_down, gz_up, gz_down]
    barrier = pltpu.get_barrier_semaphore()
    for device in everyone:
        pl.semaphore_signal(barrier, inc=1, device_id=device, device_id_type=MESH)
    pl.semaphore_wait(barrier, len(everyone))

    order = (4, 3, 5, 2, 6, 1, 7)

    def columns(j):
        return pl.ds(pl.multiple_of(j * 128, 128), 128)

    def spread(field, slot):
        copies = []
        for n, d in enumerate(order):
            j = (ta + d) % 8
            copies.append(
                remote(
                    vel.at[field, :, :, columns(j)], recv.at[field, ta],
                    a2a_s.at[slot, n], a2a_r.at[slot, n], (gx, gz, j),
                )
            )
        for copy in copies:
            copy.start()
        mine = pltpu.make_async_copy(
            vel.at[field, :, :, columns(ta)], recv.at[field, ta], loc_s.at[slot]
        )
        mine.start()
        return copies, mine

    edge_up = remote(
        vel.at[U, :, :, 896:1024], uext.at[:, :, 0:128], edge_s.at[0], edge_r.at[0], gz_up
    )
    edge_down = remote(
        vel.at[U, :, :, 0:128], uext.at[:, :, 1152:1280], edge_s.at[1], edge_r.at[1], gz_down
    )
    edge_up.start()
    edge_down.start()
    body = pltpu.make_async_copy(vel.at[U], uext.at[:, :, 128:1152], loc_s.at[3])
    body.start()
    sent_w = spread(W, 0)
    sent_u = spread(U, 1)

    for s in range(NSEG):
        o = owner[s]
        o_gx, o_gz = o // 4, o % 4
        o_x, o_y = o_gx % 4, (o_gz // 2) * 2 + o_gx // 4
        own_core[s] = o_gz % 2
        own_1[s] = (1 - core) * o_x + core * o_y
        own_2[s] = (1 - core) * o_y + core * o_x
    for i in range(PIECE):
        s = jnp.minimum((m1 * PIECE + i) // 14, NSEG - 1)
        tile_1[i] = own_1[s]
        tile_2[i] = own_2[s]

    body.wait()
    edge_up.wait_recv()
    edge_down.wait_recv()
    r_io = lax.broadcasted_iota(jnp.int32, (128, 1280), 0)
    l_io = lax.broadcasted_iota(jnp.int32, (128, 1280), 1)
    r16 = r_io % 16
    r4 = r16 % 4
    target = 128 + 128 * (r_io // 16) + r4 + jnp.where(r4 < 2, -2, 126)
    hit = l_io == target
    packed = jnp.zeros((128, 128), F32)
    for h in range(2):
        select = jnp.where(hit & (r16 // 4 == h), 1.0, 0.0).astype(BF)
        data = uext[4 * h : 4 * h + 4].reshape(128, 1280)
        packed += lax.dot_general(
            select, data, (((1,), (1,)), ((), ())), preferred_element_type=F32
        )
    hz_out[...] = packed.astype(BF).reshape(8, 16, 128)
    sent_hz = []
    for n, d in enumerate(order):
        j = (ta + d) % 8
        sent_hz.append(
            remote(hz_out.at[j], hz_in.at[ta], hz_s.at[n], hz_r.at[n], (gx, gz, j))
        )
    for copy in sent_hz:
        copy.start()
    hz_in[ta] = hz_out[ta]
    sent_v = spread(V, 2)

    col = lax.broadcasted_iota(jnp.int32, (16, 1024), 1)
    lag_io = lax.broadcasted_iota(jnp.int32, (16, 1024), 0)
    same = (
        lax.broadcasted_iota(jnp.int32, (224, 1024), 0) % 16
        == lax.broadcasted_iota(jnp.int32, (224, 1024), 1) % 16
    )

    def build(s, carry):
        one = jnp.where(col // 16 - offsets[s] == lag_io, 1.0, 0.0).astype(BF)
        full = jnp.dot(rows_ref[...], one, preferred_element_type=F32)
        wm[s] = jnp.where(same, full, 0.0).astype(BF)
        return carry

    lax.fori_loop(0, NSEG, build, 0)

    def transform(q, src):
        xs[:, 0:128] = src[:, :, 0:16, :].reshape(1024, 128)
        xs[:, 128:256] = src[:, :, 16:32, :].reshape(1024, 128)
        copies = []
        for s in range(NSEG):
            r = jnp.dot(wm[s], xs[...], preferred_element_type=F32)
            rows = slice(s * 14, s * 14 + 14)
            spec[q, rows] = r.reshape(14, 16, 256)
            lo = r[:, 0:128].astype(BF).reshape(14, 16, 128)
            hi = r[:, 128:256].astype(BF).reshape(14, 16, 128)
            c_buf[q][core, rows] = jnp.where(core == 0, lo, hi)
            a_buf[q, rows] = jnp.where(core == 0, hi, lo)
            copy = remote(
                a_buf.at[q, rows], c_buf[q].at[core, rows],
                core_s.at[q, s], core_r.at[q, s], partner,
            )
            copy.start()
            copies.append(copy)
        return copies

    def scatter(q, before):
        for s, copy in enumerate(before):
            copy.wait_recv()
        for s in range(NSEG):
            d_buf[q, s * 14 : s * 14 + 14] = c_buf[q][own_core[s], s * 14 : s * 14 + 14]
        d_buf[q, J:TILES] = jnp.zeros((2, 16, 128), BF)
        copies = []
        for d in (2, 1, 3):
            p, device = peer_1(d)
            copies.append(
                remote(
                    d_buf.at[q, pl.ds(p * PIECE, PIECE)], e_buf[q].at[m1],
                    l1_s.at[q, d - 1], l1_r.at[q, d - 1], device,
                )
            )
        for copy in copies:
            copy.start()
        e_buf[q][m1] = d_buf[q, pl.ds(m1 * PIECE, PIECE)]
        return copies

    def exchange(q, before):
        for copy in before:
            copy.wait_recv()
        for i in range(PIECE):
            f_buf[q, i] = e_buf[q][tile_1[i], i]
        copies = []
        for d in (2, 1, 3):
            copies.append(
                remote(
                    f_buf.at[q], g_buf[q].at[m2],
                    l2_s.at[q, d - 1], l2_r.at[q, d - 1], peer_2(d)[1],
                )
            )
        for copy in copies:
            copy.start()
        g_buf[q][m2] = f_buf[q]
        return copies

    def piece_of(q, p):
        return t_buf.at[q, core, pl.ds(p * PIECE, PIECE)]

    def gather(q, before):
        for copy in before:
            copy.wait_recv()
        for i in range(PIECE):
            t_buf[q, core, m1 * PIECE + i] = g_buf[q][tile_2[i], i]
        copies = []
        for d in (2, 1, 3):
            copies.append(
                remote(
                    piece_of(q, m1), piece_of(q, m1),
                    g1_s.at[q, d - 1], g1_r.at[q, d - 1], peer_1(d)[1],
                )
            )
        for copy in copies:
            copy.start()
        mine = remote(piece_of(q, m1), piece_of(q, m1), gc_s.at[q, 0], gc_r.at[q, 0], partner)
        mine.start()
        return [mine] + copies

    def share(q, before):
        copies = [before[0]]
        for n, d in ((2, 1), (3, 3), (1, 2)):
            before[n].wait_recv()
            p = (m1 + 4 - d) % 4
            copy = remote(piece_of(q, p), piece_of(q, p), gc_s.at[q, d], gc_r.at[q, d], partner)
            copy.start()
            copies.append(copy)
        forwarded.extend(copies[1:])
        return copies

    scaling = 8.0 / (3.0 * SEG * NSEG)

    def finish(q, before):
        for copy in before:
            copy.wait_recv()

        def one_frequency(k, carry):
            for h in range(2):
                co = jnp.zeros((16, 128), F32)
                quad = jnp.zeros((16, 128), F32)
                for s in range(NSEG):
                    rc = t_buf[q, h, s * 14 + k].astype(F32)
                    rs = t_buf[q, h, s * 14 + F + k].astype(F32)
                    lc = spec[q, s * 14 + k, :, h * 128 : h * 128 + 128]
                    ls = spec[q, s * 14 + F + k, :, h * 128 : h * 128 + 128]
                    co += rc * lc + rs * ls
                    quad += rc * ls - rs * lc
                out_v[q, 0, k, h * 16 : h * 16 + 16, :] = co * scaling
                out_v[q, 1, k, h * 16 : h * 16 + 16, :] = quad * scaling
            return carry

        lax.fori_loop(0, F, one_frequency, 0)
        copy = pltpu.make_async_copy(out_v.at[q], out.at[q], out_s.at[q])
        copy.start()
        return copy

    def vorticity(i, carry):
        u_i = recv[U, i].reshape(256, 128)
        w_i = jnp.concatenate(
            [recv[W, i].reshape(256, 128), h_lo[i].reshape(128, 128), h_hi[i].reshape(128, 128)],
            axis=0,
        )
        across = jnp.dot(dx_ref[...], w_i, preferred_element_type=F32)
        inner = jnp.dot(u_i, dz_ref[...], preferred_element_type=F32)
        outer = jnp.concatenate(
            [
                lax.dot_general(
                    hz_in[i], bz_ref[h], (((0,), (0,)), ((), ())), preferred_element_type=F32
                )
                for h in range(2)
            ],
            axis=0,
        )
        om[i] = ((inner + outer - across) / 12.0).astype(BF).reshape(8, 32, 128)
        return carry

    started = []
    forwarded = []
    chain = {}

    def run(step, q):
        chain[q] = step(q, chain.get(q))
        if step is not share:
            started.extend(chain[q])

    def arrived(sent):
        copies, mine = sent
        mine.wait()
        for copy in copies:
            copy.wait_recv()

    outs = []
    arrived(sent_w)
    halo_up = remote(recv.at[W, :, :, 16:32], h_lo, halo_s.at[0], halo_r.at[0], gx_up)
    halo_down = remote(recv.at[W, :, :, 0:16], h_hi, halo_s.at[1], halo_r.at[1], gx_down)
    halo_up.start()
    halo_down.start()
    chain[W] = recv.at[W]
    run(transform, W)
    for step in (scatter, exchange, gather, share):
        run(step, W)
    arrived(sent_u)
    chain[U] = recv.at[U]
    run(transform, U)
    for copy in sent_hz:
        copy.wait_recv()
    halo_up.wait_recv()
    halo_down.wait_recv()
    lax.fori_loop(0, 8, vorticity, 0)
    run(scatter, U)
    chain[OM] = om
    run(transform, OM)
    run(exchange, U)
    run(scatter, OM)
    run(gather, U)
    run(exchange, OM)
    run(share, U)
    run(gather, OM)
    outs.append(finish(W, chain[W]))
    arrived(sent_v)
    chain[V] = recv.at[V]
    run(transform, V)
    run(share, OM)
    run(scatter, V)
    outs.append(finish(U, chain[U]))
    run(exchange, V)
    outs.append(finish(OM, chain[OM]))
    run(gather, V)
    run(share, V)
    outs.append(finish(V, chain[V]))

    for copies, _ in (sent_w, sent_u, sent_v):
        for copy in copies:
            copy.wait_send()
    for copy in sent_hz + started + forwarded + [edge_up, edge_down, halo_up, halo_down]:
        copy.wait_send()
    for copy in outs:
        copy.wait()


def shards(velocity, offsets, owner):
    along_z, halo_z, along_x = slope_tables()
    dma = pltpu.SemaphoreType.DMA
    vmem = lambda *shape: pltpu.VMEM(shape, BF)
    scratch = [
        vmem(3, 8, 8, 32, 128), vmem(8, 32, 1280), vmem(8, 16, 128), vmem(8, 16, 128),
        vmem(8, 8, 16, 128), vmem(8, 8, 16, 128), vmem(8, 8, 32, 128),
        vmem(NSEG, 224, 1024), vmem(1024, 256), pltpu.VMEM((4, J, 16, 256), F32),
        vmem(4, TILES, 16, 128), *[vmem(2, TILES, 16, 128)] * 4, vmem(4, TILES, 16, 128),
        *[vmem(4, PIECE, 16, 128)] * 4, vmem(4, PIECE, 16, 128), *[vmem(4, PIECE, 16, 128)] * 4,
        vmem(4, 2, TILES, 16, 128),
        pltpu.VMEM((4, 2, F, 32, 128), F32),
        *[pltpu.SMEM((NSEG,), jnp.int32)] * 3, *[pltpu.SMEM((PIECE,), jnp.int32)] * 2,
        dma((3, 7)), dma((3, 7)), dma((7,)), dma((7,)), dma((2,)), dma((2,)), dma((2,)), dma((2,)),
        dma((4, NSEG)), dma((4, NSEG)), dma((4, 3)), dma((4, 3)), dma((4, 3)), dma((4, 3)),
        dma((4, 3)), dma((4, 3)), dma((4, 4)), dma((4, 4)),
        dma((4,)), dma((4,)),
    ]
    return pl.pallas_call(
        kernel,
        out_shape=jax.ShapeDtypeStruct((4, 2, F, 32, 128), F32),
        in_specs=[
            pl.BlockSpec(memory_space=pl.ANY),
            pl.BlockSpec(memory_space=pltpu.SMEM),
            pl.BlockSpec(memory_space=pltpu.SMEM),
        ]
        + [pl.BlockSpec(memory_space=pltpu.VMEM)] * 4,
        out_specs=pl.BlockSpec(memory_space=pl.ANY),
        scratch_shapes=scratch,
        compiler_params=pltpu.CompilerParams(
            collective_id=0, has_side_effects=True, vmem_limit_bytes=56 << 20
        ),
        name="cross_spectra",
    )(
        velocity, offsets, owner, jnp.asarray(table_rows()), jnp.asarray(along_z),
        jnp.asarray(halo_z), jnp.asarray(along_x),
    )


def solution(mesh):
    in_specs = (P(None, "ta", "gx", "gz"), P(), P())
    out_specs = P(None, None, None, "gx", ("gz", "ta"))
    return jax.shard_map(shards, mesh=mesh, in_specs=in_specs, out_specs=out_specs, check_vma=False)
```

```python
import math

import jax
import jax.numpy as jnp
import numpy as np
from jax import lax
from jax.experimental import pallas as pl
from jax.experimental.pallas import tpu as pltpu
from jax.sharding import PartitionSpec as P

SEG = 16
NSEG = 7
F = 7
J = NSEG * 2 * F
TILES = 100
PIECE = 25
MESH = pl.DeviceIdType.MESH
U, V, W, OM = 0, 1, 2, 3
BF = jnp.bfloat16
F32 = jnp.float32
ORDER = (
    "wT", "wA", "wB", "uT", "wG", "uA", "oT", "wH", "uB", "oA", "vT", "vA",
    "uG", "oB", "vB", "uH", "oG", "wF", "vG", "uF", "oH", "oF", "vH", "vF",
)


def table_rows():
    lag = np.arange(SEG)
    window = 0.5 - 0.5 * np.cos(2.0 * math.pi / SEG * lag)
    turns = np.arange(1, F + 1)[:, None] * lag[None, :] % SEG
    phase = 2.0 * math.pi / SEG * turns
    rows = np.concatenate([window * np.cos(phase), -window * np.sin(phase)], axis=0)
    rows = rows.astype(np.float32).astype(jnp.bfloat16)
    return np.repeat(rows, 16, axis=0)


def slope(delta):
    out = np.zeros(delta.shape, np.float32)
    for shift, coefficient in ((1, 8.0), (-1, -8.0), (2, -1.0), (-2, 1.0)):
        out[delta == shift] = coefficient
    return out


def slope_tables():
    lane = np.arange(128)
    along_z = slope(lane[:, None] - lane[None, :])
    edge = np.array([-2, -1, 128, 129])
    edge_rows = slope(edge[:, None] - lane[None, :])
    halo_z = np.zeros((2, 16, 128), np.float32)
    halo_z[0, 0:4] = edge_rows
    halo_z[1, 4:8] = edge_rows
    snap_out = np.repeat(np.arange(8), 32)
    row_out = np.tile(np.arange(32), 8)
    snap_half = np.repeat(np.arange(8), 16)
    row_half = np.tile(np.arange(16), 8)
    snap_in = np.concatenate([snap_out, snap_half, snap_half])
    row_in = np.concatenate([row_out, row_half - 16, row_half + 32])
    along_x = slope(row_in[None, :] - row_out[:, None])
    along_x = along_x * (snap_in[None, :] == snap_out[:, None])
    cast = lambda a: a.astype(jnp.bfloat16)
    return cast(along_z), cast(halo_z), cast(along_x)


def kernel(
    vel, offsets, owner, rows_ref, dz_ref, bz_ref, dx_ref, out,
    recv, uext, hz_out, hz_in, h_lo, h_hi, om, wm, xs, spec,
    a_buf, c_0, c_1, c_2, c_3, d_buf, e_0, e_1, e_2, e_3, f_buf, g_0, g_1, g_2, g_3, t_buf, out_v,
    own_core, own_1, own_2, tile_1, tile_2,
    a2a_s, a2a_r, hz_s, hz_r, edge_s, edge_r, halo_s, halo_r,
    core_s, core_r, l1_s, l1_r, l2_s, l2_r, g1_s, g1_r, gc_s, gc_r,
    loc_s, out_s,
):
    c_buf, e_buf, g_buf = (c_0, c_1, c_2, c_3), (e_0, e_1, e_2, e_3), (g_0, g_1, g_2, g_3)
    gx, gz, ta = lax.axis_index("gx"), lax.axis_index("gz"), lax.axis_index("ta")
    core = gz % 2
    x = gx % 4
    y = (gz // 2) * 2 + gx // 4

    def chip(px, py, pc):
        return ((py % 2) * 4 + px, (py // 2) * 2 + pc, ta)

    m1 = (1 - core) * x + core * y
    m2 = (1 - core) * y + core * x

    def peer_1(step):
        p = (m1 + step) % 4
        return p, chip((1 - core) * p + core * x, (1 - core) * y + core * p, core)

    def peer_2(step):
        p = (m2 + step) % 4
        return p, chip((1 - core) * x + core * p, (1 - core) * p + core * y, core)

    partner = (gx, (gz // 2) * 2 + 1 - core, ta)
    gx_up, gx_down = ((gx + 1) % 8, gz, ta), ((gx + 7) % 8, gz, ta)
    gz_up, gz_down = (gx, (gz + 1) % 4, ta), (gx, (gz + 3) % 4, ta)

    def remote(src, dst, send, recv_sem, device):
        return pltpu.make_async_remote_copy(
            src_ref=src, dst_ref=dst, send_sem=send, recv_sem=recv_sem,
            device_id=device, device_id_type=MESH,
        )

    everyone = [(gx, gz, (ta + d) % 8) for d in range(1, 8)]
    everyone += [peer_1(d)[1] for d in (1, 2, 3)] + [peer_2(d)[1] for d in (1, 2, 3)]
    everyone += [partner, gx_up, gx_down, gz_up, gz_down]
    barrier = pltpu.get_barrier_semaphore()
    for device in everyone:
        pl.semaphore_signal(barrier, inc=1, device_id=device, device_id_type=MESH)
    pl.semaphore_wait(barrier, len(everyone))

    order = (4, 3, 5, 2, 6, 1, 7)

    def columns(j):
        return pl.ds(pl.multiple_of(j * 128, 128), 128)

    def spread(field, slot):
        copies = []
        for n, d in enumerate(order):
            j = (ta + d) % 8
            copies.append(
                remote(
                    vel.at[field, :, :, columns(j)], recv.at[field, ta],
                    a2a_s.at[slot, n], a2a_r.at[slot, n], (gx, gz, j),
                )
            )
        for copy in copies:
            copy.start()
        mine = pltpu.make_async_copy(
            vel.at[field, :, :, columns(ta)], recv.at[field, ta], loc_s.at[slot]
        )
        mine.start()
        return copies, mine

    edge_up = remote(
        vel.at[U, :, :, 896:1024], uext.at[:, :, 0:128], edge_s.at[0], edge_r.at[0], gz_up
    )
    edge_down = remote(
        vel.at[U, :, :, 0:128], uext.at[:, :, 1152:1280], edge_s.at[1], edge_r.at[1], gz_down
    )
    edge_up.start()
    edge_down.start()
    body = pltpu.make_async_copy(vel.at[U], uext.at[:, :, 128:1152], loc_s.at[3])
    body.start()
    sent_w = spread(W, 0)
    sent_u = spread(U, 1)

    for s in range(NSEG):
        o = owner[s]
        o_gx, o_gz = o // 4, o % 4
        o_x, o_y = o_gx % 4, (o_gz // 2) * 2 + o_gx // 4
        own_core[s] = o_gz % 2
        own_1[s] = (1 - core) * o_x + core * o_y
        own_2[s] = (1 - core) * o_y + core * o_x
    for i in range(PIECE):
        s = jnp.minimum((m1 * PIECE + i) // 14, NSEG - 1)
        tile_1[i] = own_1[s]
        tile_2[i] = own_2[s]

    body.wait()
    edge_up.wait_recv()
    edge_down.wait_recv()
    r_io = lax.broadcasted_iota(jnp.int32, (128, 1280), 0)
    l_io = lax.broadcasted_iota(jnp.int32, (128, 1280), 1)
    r16 = r_io % 16
    r4 = r16 % 4
    target = 128 + 128 * (r_io // 16) + r4 + jnp.where(r4 < 2, -2, 126)
    hit = l_io == target
    packed = jnp.zeros((128, 128), F32)
    for h in range(2):
        select = jnp.where(hit & (r16 // 4 == h), 1.0, 0.0).astype(BF)
        data = uext[4 * h : 4 * h + 4].reshape(128, 1280)
        packed += lax.dot_general(
            select, data, (((1,), (1,)), ((), ())), preferred_element_type=F32
        )
    hz_out[...] = packed.astype(BF).reshape(8, 16, 128)
    sent_hz = []
    for n, d in enumerate(order):
        j = (ta + d) % 8
        sent_hz.append(
            remote(hz_out.at[j], hz_in.at[ta], hz_s.at[n], hz_r.at[n], (gx, gz, j))
        )
    for copy in sent_hz:
        copy.start()
    hz_in[ta] = hz_out[ta]
    sent_v = spread(V, 2)

    col = lax.broadcasted_iota(jnp.int32, (16, 1024), 1)
    lag_io = lax.broadcasted_iota(jnp.int32, (16, 1024), 0)
    same = (
        lax.broadcasted_iota(jnp.int32, (224, 1024), 0) % 16
        == lax.broadcasted_iota(jnp.int32, (224, 1024), 1) % 16
    )

    def build(s, carry):
        one = jnp.where(col // 16 - offsets[s] == lag_io, 1.0, 0.0).astype(BF)
        full = jnp.dot(rows_ref[...], one, preferred_element_type=F32)
        wm[s] = jnp.where(same, full, 0.0).astype(BF)
        return carry

    lax.fori_loop(0, NSEG, build, 0)

    def transform(q, src):
        xs[:, 0:128] = src[:, :, 0:16, :].reshape(1024, 128)
        xs[:, 128:256] = src[:, :, 16:32, :].reshape(1024, 128)
        copies = []
        for s in range(NSEG):
            r = jnp.dot(wm[s], xs[...], preferred_element_type=F32)
            rows = slice(s * 14, s * 14 + 14)
            spec[q, rows] = r.reshape(14, 16, 256)
            lo = r[:, 0:128].astype(BF).reshape(14, 16, 128)
            hi = r[:, 128:256].astype(BF).reshape(14, 16, 128)
            c_buf[q][core, rows] = jnp.where(core == 0, lo, hi)
            a_buf[q, rows] = jnp.where(core == 0, hi, lo)
            copy = remote(
                a_buf.at[q, rows], c_buf[q].at[core, rows],
                core_s.at[q, s], core_r.at[q, s], partner,
            )
            copy.start()
            copies.append(copy)
        return copies

    def scatter(q, before):
        for s, copy in enumerate(before):
            copy.wait_recv()
        for s in range(NSEG):
            d_buf[q, s * 14 : s * 14 + 14] = c_buf[q][own_core[s], s * 14 : s * 14 + 14]
        d_buf[q, J:TILES] = jnp.zeros((2, 16, 128), BF)
        copies = []
        for d in (2, 1, 3):
            p, device = peer_1(d)
            copies.append(
                remote(
                    d_buf.at[q, pl.ds(p * PIECE, PIECE)], e_buf[q].at[m1],
                    l1_s.at[q, d - 1], l1_r.at[q, d - 1], device,
                )
            )
        for copy in copies:
            copy.start()
        e_buf[q][m1] = d_buf[q, pl.ds(m1 * PIECE, PIECE)]
        return copies

    def exchange(q, before):
        for copy in before:
            copy.wait_recv()
        for i in range(PIECE):
            f_buf[q, i] = e_buf[q][tile_1[i], i]
        copies = []
        for d in (2, 1, 3):
            copies.append(
                remote(
                    f_buf.at[q], g_buf[q].at[m2],
                    l2_s.at[q, d - 1], l2_r.at[q, d - 1], peer_2(d)[1],
                )
            )
        for copy in copies:
            copy.start()
        g_buf[q][m2] = f_buf[q]
        return copies

    def piece_of(q, p):
        return t_buf.at[q, core, pl.ds(p * PIECE, PIECE)]

    def gather(q, before):
        for copy in before:
            copy.wait_recv()
        for i in range(PIECE):
            t_buf[q, core, m1 * PIECE + i] = g_buf[q][tile_2[i], i]
        copies = []
        for d in (2, 1, 3):
            copies.append(
                remote(
                    piece_of(q, m1), piece_of(q, m1),
                    g1_s.at[q, d - 1], g1_r.at[q, d - 1], peer_1(d)[1],
                )
            )
        for copy in copies:
            copy.start()
        mine = remote(piece_of(q, m1), piece_of(q, m1), gc_s.at[q, 0], gc_r.at[q, 0], partner)
        mine.start()
        return [mine] + copies

    def share(q, before):
        copies = [before[0]]
        for n, d in ((2, 1), (3, 3), (1, 2)):
            before[n].wait_recv()
            p = (m1 + 4 - d) % 4
            copy = remote(piece_of(q, p), piece_of(q, p), gc_s.at[q, d], gc_r.at[q, d], partner)
            copy.start()
            copies.append(copy)
        forwarded.extend(copies[1:])
        return copies

    scaling = 8.0 / (3.0 * SEG * NSEG)

    def finish(q, before):
        for copy in before:
            copy.wait_recv()

        def one_frequency(k, carry):
            for h in range(2):
                co = jnp.zeros((16, 128), F32)
                quad = jnp.zeros((16, 128), F32)
                for s in range(NSEG):
                    rc = t_buf[q, h, s * 14 + k].astype(F32)
                    rs = t_buf[q, h, s * 14 + F + k].astype(F32)
                    lc = spec[q, s * 14 + k, :, h * 128 : h * 128 + 128]
                    ls = spec[q, s * 14 + F + k, :, h * 128 : h * 128 + 128]
                    co += rc * lc + rs * ls
                    quad += rc * ls - rs * lc
                out_v[q, 0, k, h * 16 : h * 16 + 16, :] = co * scaling
                out_v[q, 1, k, h * 16 : h * 16 + 16, :] = quad * scaling
            return carry

        lax.fori_loop(0, F, one_frequency, 0)
        copy = pltpu.make_async_copy(out_v.at[q], out.at[q], out_s.at[q])
        copy.start()
        return copy

    def vorticity(i, carry):
        u_i = recv[U, i].reshape(256, 128)
        w_i = jnp.concatenate(
            [recv[W, i].reshape(256, 128), h_lo[i].reshape(128, 128), h_hi[i].reshape(128, 128)],
            axis=0,
        )
        across = jnp.dot(dx_ref[...], w_i, preferred_element_type=F32)
        inner = jnp.dot(u_i, dz_ref[...], preferred_element_type=F32)
        outer = jnp.concatenate(
            [
                lax.dot_general(
                    hz_in[i], bz_ref[h], (((0,), (0,)), ((), ())), preferred_element_type=F32
                )
                for h in range(2)
            ],
            axis=0,
        )
        om[i] = ((inner + outer - across) / 12.0).astype(BF).reshape(8, 32, 128)
        return carry

    started = []
    forwarded = []
    chain = {}

    def run(step, q):
        chain[q] = step(q, chain.get(q))
        if step is not share:
            started.extend(chain[q])

    def arrived(sent):
        copies, mine = sent
        mine.wait()
        for copy in copies:
            copy.wait_recv()

    outs = []
    halo = [
        remote(recv.at[W, :, :, 16:32], h_lo, halo_s.at[0], halo_r.at[0], gx_up),
        remote(recv.at[W, :, :, 0:16], h_hi, halo_s.at[1], halo_r.at[1], gx_down),
    ]
    quantity = {"u": U, "v": V, "w": W, "o": OM}
    steps = {"A": scatter, "B": exchange, "G": gather, "H": share}
    sent = {U: sent_u, V: sent_v, W: sent_w}
    for token in ORDER:
        q, step = quantity[token[0]], token[1]
        if step == "T":
            if q == OM:
                for copy in sent_hz + halo:
                    copy.wait_recv()
                lax.fori_loop(0, 8, vorticity, 0)
                chain[q] = om
            else:
                arrived(sent[q])
                if q == W:
                    for copy in halo:
                        copy.start()
                chain[q] = recv.at[q]
            run(transform, q)
        elif step == "F":
            outs.append(finish(q, chain[q]))
        else:
            run(steps[step], q)

    for copies, _ in (sent_w, sent_u, sent_v):
        for copy in copies:
            copy.wait_send()
    for copy in sent_hz + started + forwarded + halo + [edge_up, edge_down]:
        copy.wait_send()
    for copy in outs:
        copy.wait()


def shards(velocity, offsets, owner):
    along_z, halo_z, along_x = slope_tables()
    dma = pltpu.SemaphoreType.DMA
    vmem = lambda *shape: pltpu.VMEM(shape, BF)
    scratch = [
        vmem(3, 8, 8, 32, 128), vmem(8, 32, 1280), vmem(8, 16, 128), vmem(8, 16, 128),
        vmem(8, 8, 16, 128), vmem(8, 8, 16, 128), vmem(8, 8, 32, 128),
        vmem(NSEG, 224, 1024), vmem(1024, 256), pltpu.VMEM((4, J, 16, 256), F32),
        vmem(4, TILES, 16, 128), *[vmem(2, TILES, 16, 128)] * 4, vmem(4, TILES, 16, 128),
        *[vmem(4, PIECE, 16, 128)] * 4, vmem(4, PIECE, 16, 128), *[vmem(4, PIECE, 16, 128)] * 4,
        vmem(4, 2, TILES, 16, 128),
        pltpu.VMEM((4, 2, F, 32, 128), F32),
        *[pltpu.SMEM((NSEG,), jnp.int32)] * 3, *[pltpu.SMEM((PIECE,), jnp.int32)] * 2,
        dma((3, 7)), dma((3, 7)), dma((7,)), dma((7,)), dma((2,)), dma((2,)), dma((2,)), dma((2,)),
        dma((4, NSEG)), dma((4, NSEG)), dma((4, 3)), dma((4, 3)), dma((4, 3)), dma((4, 3)),
        dma((4, 3)), dma((4, 3)), dma((4, 4)), dma((4, 4)),
        dma((4,)), dma((4,)),
    ]
    return pl.pallas_call(
        kernel,
        out_shape=jax.ShapeDtypeStruct((4, 2, F, 32, 128), F32),
        in_specs=[
            pl.BlockSpec(memory_space=pl.ANY),
            pl.BlockSpec(memory_space=pltpu.SMEM),
            pl.BlockSpec(memory_space=pltpu.SMEM),
        ]
        + [pl.BlockSpec(memory_space=pltpu.VMEM)] * 4,
        out_specs=pl.BlockSpec(memory_space=pl.ANY),
        scratch_shapes=scratch,
        compiler_params=pltpu.CompilerParams(
            collective_id=0, has_side_effects=True, vmem_limit_bytes=56 << 20
        ),
        name="cross_spectra",
    )(
        velocity, offsets, owner, jnp.asarray(table_rows()), jnp.asarray(along_z),
        jnp.asarray(halo_z), jnp.asarray(along_x),
    )


def solution(mesh):
    in_specs = (P(None, "ta", "gx", "gz"), P(), P())
    out_specs = P(None, None, None, "gx", ("gz", "ta"))
    return jax.shard_map(shards, mesh=mesh, in_specs=in_specs, out_specs=out_specs, check_vma=False)
```

```python
import math

import jax
import jax.numpy as jnp
import numpy as np
from jax import lax
from jax.experimental import pallas as pl
from jax.experimental.pallas import tpu as pltpu
from jax.sharding import PartitionSpec as P

SEG = 16
NSEG = 7
F = 7
J = NSEG * 2 * F
TILES = 100
PIECE = 25
MESH = pl.DeviceIdType.MESH
U, V, W, OM = 0, 1, 2, 3
BF = jnp.bfloat16
F32 = jnp.float32
ORDER = (
    "wT", "wA", "wB", "uT", "wG", "uA", "oT", "wH", "uB", "oA", "vT", "vA",
    "uG", "vB", "oB", "vG", "uH", "oG", "wF", "uF", "vH", "oH", "oF", "vF",
)


def table_rows():
    lag = np.arange(SEG)
    window = 0.5 - 0.5 * np.cos(2.0 * math.pi / SEG * lag)
    turns = np.arange(1, F + 1)[:, None] * lag[None, :] % SEG
    phase = 2.0 * math.pi / SEG * turns
    rows = np.concatenate([window * np.cos(phase), -window * np.sin(phase)], axis=0)
    rows = rows.astype(np.float32).astype(jnp.bfloat16)
    return np.repeat(rows, 16, axis=0)


def slope(delta):
    out = np.zeros(delta.shape, np.float32)
    for shift, coefficient in ((1, 8.0), (-1, -8.0), (2, -1.0), (-2, 1.0)):
        out[delta == shift] = coefficient
    return out


def slope_tables():
    lane = np.arange(128)
    along_z = slope(lane[:, None] - lane[None, :])
    edge = np.array([-2, -1, 128, 129])
    edge_rows = slope(edge[:, None] - lane[None, :])
    halo_z = np.zeros((2, 16, 128), np.float32)
    halo_z[0, 0:4] = edge_rows
    halo_z[1, 4:8] = edge_rows
    snap_out = np.repeat(np.arange(8), 32)
    row_out = np.tile(np.arange(32), 8)
    snap_edge = np.repeat(np.arange(8), 2)
    row_edge = np.tile(np.arange(2), 8)
    snap_in = np.concatenate([snap_out, snap_edge, snap_edge])
    row_in = np.concatenate([row_out, row_edge - 2, row_edge + 32])
    snap_sent = np.concatenate([snap_edge, snap_edge])
    row_sent = np.concatenate([row_edge + 30, row_edge])
    sent = snap_sent[:, None] == snap_out[None, :]
    sent = (sent & (row_sent[:, None] == row_out[None, :])).astype(np.float32)
    along_x = slope(row_in[None, :] - row_out[:, None])
    along_x = along_x * (snap_in[None, :] == snap_out[:, None])
    cast = lambda a: a.astype(jnp.bfloat16)
    return cast(along_z), cast(halo_z), cast(along_x), cast(sent)


def kernel(
    vel, offsets, owner, rows_ref, dz_ref, bz_ref, dx_ref, sent_ref, out,
    recv, uext, hz_out, hz_in, h_up, h_down, h_lo, h_hi, om, wm, xs, spec,
    a_buf, c_0, c_1, c_2, c_3, d_buf, e_0, e_1, e_2, e_3, f_buf, g_0, g_1, g_2, g_3, t_buf, out_v,
    own_core, own_1, own_2, tile_1, tile_2,
    a2a_s, a2a_r, hz_s, hz_r, edge_s, edge_r, halo_s, halo_r,
    core_s, core_r, l1_s, l1_r, l2_s, l2_r, g1_s, g1_r, gc_s, gc_r,
    loc_s, out_s,
):
    c_buf, e_buf, g_buf = (c_0, c_1, c_2, c_3), (e_0, e_1, e_2, e_3), (g_0, g_1, g_2, g_3)
    gx, gz, ta = lax.axis_index("gx"), lax.axis_index("gz"), lax.axis_index("ta")
    core = gz % 2
    x = gx % 4
    y = (gz // 2) * 2 + gx // 4

    def chip(px, py, pc):
        return ((py % 2) * 4 + px, (py // 2) * 2 + pc, ta)

    m1 = (1 - core) * x + core * y
    m2 = (1 - core) * y + core * x

    def peer_1(step):
        p = (m1 + step) % 4
        return p, chip((1 - core) * p + core * x, (1 - core) * y + core * p, core)

    def peer_2(step):
        p = (m2 + step) % 4
        return p, chip((1 - core) * x + core * p, (1 - core) * p + core * y, core)

    partner = (gx, (gz // 2) * 2 + 1 - core, ta)
    gx_up, gx_down = ((gx + 1) % 8, gz, ta), ((gx + 7) % 8, gz, ta)
    gz_up, gz_down = (gx, (gz + 1) % 4, ta), (gx, (gz + 3) % 4, ta)

    def remote(src, dst, send, recv_sem, device):
        return pltpu.make_async_remote_copy(
            src_ref=src, dst_ref=dst, send_sem=send, recv_sem=recv_sem,
            device_id=device, device_id_type=MESH,
        )

    everyone = [(gx, gz, (ta + d) % 8) for d in range(1, 8)]
    everyone += [peer_1(d)[1] for d in (1, 2, 3)] + [peer_2(d)[1] for d in (1, 2, 3)]
    everyone += [partner, gx_up, gx_down, gz_up, gz_down]
    barrier = pltpu.get_barrier_semaphore()
    for device in everyone:
        pl.semaphore_signal(barrier, inc=1, device_id=device, device_id_type=MESH)
    pl.semaphore_wait(barrier, len(everyone))

    order = (4, 3, 5, 2, 6, 1, 7)

    def columns(j):
        return pl.ds(pl.multiple_of(j * 128, 128), 128)

    def spread(field, slot):
        copies = []
        for n, d in enumerate(order):
            j = (ta + d) % 8
            copies.append(
                remote(
                    vel.at[field, :, :, columns(j)], recv.at[field, ta],
                    a2a_s.at[slot, n], a2a_r.at[slot, n], (gx, gz, j),
                )
            )
        for copy in copies:
            copy.start()
        mine = pltpu.make_async_copy(
            vel.at[field, :, :, columns(ta)], recv.at[field, ta], loc_s.at[slot]
        )
        mine.start()
        return copies, mine

    edge_up = remote(
        vel.at[U, :, :, 896:1024], uext.at[:, :, 0:128], edge_s.at[0], edge_r.at[0], gz_up
    )
    edge_down = remote(
        vel.at[U, :, :, 0:128], uext.at[:, :, 1152:1280], edge_s.at[1], edge_r.at[1], gz_down
    )
    edge_up.start()
    edge_down.start()
    body = pltpu.make_async_copy(vel.at[U], uext.at[:, :, 128:1152], loc_s.at[3])
    body.start()
    sent_w = spread(W, 0)
    sent_u = spread(U, 1)

    for s in range(NSEG):
        o = owner[s]
        o_gx, o_gz = o // 4, o % 4
        o_x, o_y = o_gx % 4, (o_gz // 2) * 2 + o_gx // 4
        own_core[s] = o_gz % 2
        own_1[s] = (1 - core) * o_x + core * o_y
        own_2[s] = (1 - core) * o_y + core * o_x
    for i in range(PIECE):
        s = jnp.minimum((m1 * PIECE + i) // 14, NSEG - 1)
        tile_1[i] = own_1[s]
        tile_2[i] = own_2[s]

    body.wait()
    edge_up.wait_recv()
    edge_down.wait_recv()
    r_io = lax.broadcasted_iota(jnp.int32, (128, 1280), 0)
    l_io = lax.broadcasted_iota(jnp.int32, (128, 1280), 1)
    r16 = r_io % 16
    r4 = r16 % 4
    target = 128 + 128 * (r_io // 16) + r4 + jnp.where(r4 < 2, -2, 126)
    hit = l_io == target
    packed = jnp.zeros((128, 128), F32)
    for h in range(2):
        select = jnp.where(hit & (r16 // 4 == h), 1.0, 0.0).astype(BF)
        data = uext[4 * h : 4 * h + 4].reshape(128, 1280)
        packed += lax.dot_general(
            select, data, (((1,), (1,)), ((), ())), preferred_element_type=F32
        )
    hz_out[...] = packed.astype(BF).reshape(8, 16, 128)
    sent_hz = []
    for n, d in enumerate(order):
        j = (ta + d) % 8
        sent_hz.append(
            remote(hz_out.at[j], hz_in.at[ta], hz_s.at[n], hz_r.at[n], (gx, gz, j))
        )
    for copy in sent_hz:
        copy.start()
    hz_in[ta] = hz_out[ta]
    sent_v = spread(V, 2)

    col = lax.broadcasted_iota(jnp.int32, (16, 1024), 1)
    lag_io = lax.broadcasted_iota(jnp.int32, (16, 1024), 0)
    same = (
        lax.broadcasted_iota(jnp.int32, (224, 1024), 0) % 16
        == lax.broadcasted_iota(jnp.int32, (224, 1024), 1) % 16
    )

    def build(s, carry):
        one = jnp.where(col // 16 - offsets[s] == lag_io, 1.0, 0.0).astype(BF)
        full = jnp.dot(rows_ref[...], one, preferred_element_type=F32)
        wm[s] = jnp.where(same, full, 0.0).astype(BF)
        return carry

    lax.fori_loop(0, NSEG, build, 0)

    def transform(q, src):
        xs[:, 0:128] = src[:, :, 0:16, :].reshape(1024, 128)
        xs[:, 128:256] = src[:, :, 16:32, :].reshape(1024, 128)
        copies = []
        for s in range(NSEG):
            r = jnp.dot(wm[s], xs[...], preferred_element_type=F32)
            rows = slice(s * 14, s * 14 + 14)
            spec[q, rows] = r.reshape(14, 16, 256)
            lo = r[:, 0:128].astype(BF).reshape(14, 16, 128)
            hi = r[:, 128:256].astype(BF).reshape(14, 16, 128)
            c_buf[q][core, rows] = jnp.where(core == 0, lo, hi)
            a_buf[q, rows] = jnp.where(core == 0, hi, lo)
            copy = remote(
                a_buf.at[q, rows], c_buf[q].at[core, rows],
                core_s.at[q, s], core_r.at[q, s], partner,
            )
            copy.start()
            copies.append(copy)
        return copies

    def scatter(q, before):
        for s, copy in enumerate(before):
            copy.wait_recv()
        for s in range(NSEG):
            d_buf[q, s * 14 : s * 14 + 14] = c_buf[q][own_core[s], s * 14 : s * 14 + 14]
        d_buf[q, J:TILES] = jnp.zeros((2, 16, 128), BF)
        copies = []
        for d in (2, 1, 3):
            p, device = peer_1(d)
            copies.append(
                remote(
                    d_buf.at[q, pl.ds(p * PIECE, PIECE)], e_buf[q].at[m1],
                    l1_s.at[q, d - 1], l1_r.at[q, d - 1], device,
                )
            )
        for copy in copies:
            copy.start()
        e_buf[q][m1] = d_buf[q, pl.ds(m1 * PIECE, PIECE)]
        return copies

    def exchange(q, before):
        for copy in before:
            copy.wait_recv()
        for i in range(PIECE):
            f_buf[q, i] = e_buf[q][tile_1[i], i]
        copies = []
        for d in (2, 1, 3):
            copies.append(
                remote(
                    f_buf.at[q], g_buf[q].at[m2],
                    l2_s.at[q, d - 1], l2_r.at[q, d - 1], peer_2(d)[1],
                )
            )
        for copy in copies:
            copy.start()
        g_buf[q][m2] = f_buf[q]
        return copies

    def piece_of(q, p):
        return t_buf.at[q, core, pl.ds(p * PIECE, PIECE)]

    def gather(q, before):
        for copy in before:
            copy.wait_recv()
        for i in range(PIECE):
            t_buf[q, core, m1 * PIECE + i] = g_buf[q][tile_2[i], i]
        copies = []
        for d in (2, 1, 3):
            copies.append(
                remote(
                    piece_of(q, m1), piece_of(q, m1),
                    g1_s.at[q, d - 1], g1_r.at[q, d - 1], peer_1(d)[1],
                )
            )
        for copy in copies:
            copy.start()
        mine = remote(piece_of(q, m1), piece_of(q, m1), gc_s.at[q, 0], gc_r.at[q, 0], partner)
        mine.start()
        return [mine] + copies

    def share(q, before):
        copies = [before[0]]
        for n, d in ((2, 1), (3, 3), (1, 2)):
            before[n].wait_recv()
            p = (m1 + 4 - d) % 4
            copy = remote(piece_of(q, p), piece_of(q, p), gc_s.at[q, d], gc_r.at[q, d], partner)
            copy.start()
            copies.append(copy)
        forwarded.extend(copies[1:])
        return copies

    scaling = 8.0 / (3.0 * SEG * NSEG)

    def finish(q, before):
        for copy in before:
            copy.wait_recv()

        def one_frequency(k, carry):
            for h in range(2):
                co = jnp.zeros((16, 128), F32)
                quad = jnp.zeros((16, 128), F32)
                for s in range(NSEG):
                    rc = t_buf[q, h, s * 14 + k].astype(F32)
                    rs = t_buf[q, h, s * 14 + F + k].astype(F32)
                    lc = spec[q, s * 14 + k, :, h * 128 : h * 128 + 128]
                    ls = spec[q, s * 14 + F + k, :, h * 128 : h * 128 + 128]
                    co += rc * lc + rs * ls
                    quad += rc * ls - rs * lc
                out_v[q, 0, k, h * 16 : h * 16 + 16, :] = co * scaling
                out_v[q, 1, k, h * 16 : h * 16 + 16, :] = quad * scaling
            return carry

        lax.fori_loop(0, F, one_frequency, 0)
        copy = pltpu.make_async_copy(out_v.at[q], out.at[q], out_s.at[q])
        copy.start()
        return copy

    def vorticity(i, carry):
        u_i = recv[U, i].reshape(256, 128)
        w_i = jnp.concatenate(
            [recv[W, i].reshape(256, 128), h_lo[i], h_hi[i]],
            axis=0,
        )
        across = jnp.dot(dx_ref[...], w_i, preferred_element_type=F32)
        inner = jnp.dot(u_i, dz_ref[...], preferred_element_type=F32)
        outer = jnp.concatenate(
            [
                lax.dot_general(
                    hz_in[i], bz_ref[h], (((0,), (0,)), ((), ())), preferred_element_type=F32
                )
                for h in range(2)
            ],
            axis=0,
        )
        om[i] = ((inner + outer - across) / 12.0).astype(BF).reshape(8, 32, 128)
        return carry

    started = []
    forwarded = []
    chain = {}

    def run(step, q):
        chain[q] = step(q, chain.get(q))
        if step is not share:
            started.extend(chain[q])

    def arrived(sent):
        copies, mine = sent
        mine.wait()
        for copy in copies:
            copy.wait_recv()

    outs = []
    halo = [
        remote(h_up, h_lo, halo_s.at[0], halo_r.at[0], gx_up),
        remote(h_down, h_hi, halo_s.at[1], halo_r.at[1], gx_down),
    ]
    quantity = {"u": U, "v": V, "w": W, "o": OM}
    steps = {"A": scatter, "B": exchange, "G": gather, "H": share}
    sent = {U: sent_u, V: sent_v, W: sent_w}
    for token in ORDER:
        q, step = quantity[token[0]], token[1]
        if step == "T":
            if q == OM:
                for copy in sent_hz + halo:
                    copy.wait_recv()
                lax.fori_loop(0, 8, vorticity, 0)
                chain[q] = om
            else:
                arrived(sent[q])
                if q == W:
                    for i in range(8):
                        edges = jnp.dot(
                            sent_ref[...], recv[W, i].reshape(256, 128), preferred_element_type=F32
                        ).astype(BF)
                        h_up[i] = edges[0:16]
                        h_down[i] = edges[16:32]
                    for copy in halo:
                        copy.start()
                chain[q] = recv.at[q]
            run(transform, q)
        elif step == "F":
            outs.append(finish(q, chain[q]))
        else:
            run(steps[step], q)

    for copies, _ in (sent_w, sent_u, sent_v):
        for copy in copies:
            copy.wait_send()
    for copy in sent_hz + started + forwarded + halo + [edge_up, edge_down]:
        copy.wait_send()
    for copy in outs:
        copy.wait()


def shards(velocity, offsets, owner):
    along_z, halo_z, along_x, edges = slope_tables()
    dma = pltpu.SemaphoreType.DMA
    vmem = lambda *shape: pltpu.VMEM(shape, BF)
    scratch = [
        vmem(3, 8, 8, 32, 128), vmem(8, 32, 1280), vmem(8, 16, 128), vmem(8, 16, 128),
        *[vmem(8, 16, 128)] * 4, vmem(8, 8, 32, 128),
        vmem(NSEG, 224, 1024), vmem(1024, 256), pltpu.VMEM((4, J, 16, 256), F32),
        vmem(4, TILES, 16, 128), *[vmem(2, TILES, 16, 128)] * 4, vmem(4, TILES, 16, 128),
        *[vmem(4, PIECE, 16, 128)] * 4, vmem(4, PIECE, 16, 128), *[vmem(4, PIECE, 16, 128)] * 4,
        vmem(4, 2, TILES, 16, 128),
        pltpu.VMEM((4, 2, F, 32, 128), F32),
        *[pltpu.SMEM((NSEG,), jnp.int32)] * 3, *[pltpu.SMEM((PIECE,), jnp.int32)] * 2,
        dma((3, 7)), dma((3, 7)), dma((7,)), dma((7,)), dma((2,)), dma((2,)), dma((2,)), dma((2,)),
        dma((4, NSEG)), dma((4, NSEG)), dma((4, 3)), dma((4, 3)), dma((4, 3)), dma((4, 3)),
        dma((4, 3)), dma((4, 3)), dma((4, 4)), dma((4, 4)),
        dma((4,)), dma((4,)),
    ]
    return pl.pallas_call(
        kernel,
        out_shape=jax.ShapeDtypeStruct((4, 2, F, 32, 128), F32),
        in_specs=[
            pl.BlockSpec(memory_space=pl.ANY),
            pl.BlockSpec(memory_space=pltpu.SMEM),
            pl.BlockSpec(memory_space=pltpu.SMEM),
        ]
        + [pl.BlockSpec(memory_space=pltpu.VMEM)] * 5,
        out_specs=pl.BlockSpec(memory_space=pl.ANY),
        scratch_shapes=scratch,
        compiler_params=pltpu.CompilerParams(
            collective_id=0, has_side_effects=True, vmem_limit_bytes=56 << 20
        ),
        name="cross_spectra",
    )(
        velocity, offsets, owner, jnp.asarray(table_rows()), jnp.asarray(along_z),
        jnp.asarray(halo_z), jnp.asarray(along_x), jnp.asarray(edges),
    )


def solution(mesh):
    in_specs = (P(None, "ta", "gx", "gz"), P(), P())
    out_specs = P(None, None, None, "gx", ("gz", "ta"))
    return jax.shard_map(shards, mesh=mesh, in_specs=in_specs, out_specs=out_specs, check_vma=False)
```

```python
import math

import jax
import jax.numpy as jnp
import numpy as np
from jax import lax
from jax.experimental import pallas as pl
from jax.experimental.pallas import tpu as pltpu
from jax.sharding import PartitionSpec as P

SEG = 16
NSEG = 7
F = 7
J = NSEG * 2 * F
TILES = 100
PIECE = 25
MESH = pl.DeviceIdType.MESH
U, V, W, OM = 0, 1, 2, 3
BF = jnp.bfloat16
F32 = jnp.float32
ORDER = (
    "wT", "wA", "wB", "uT", "wG", "uA", "oT", "uB", "wH", "oA", "vT", "vA",
    "uG", "vB", "oB", "vG", "uH", "oG", "wF", "uF", "vH", "oH", "oF", "vF",
)


def table_rows():
    lag = np.arange(SEG)
    window = 0.5 - 0.5 * np.cos(2.0 * math.pi / SEG * lag)
    turns = np.arange(1, F + 1)[:, None] * lag[None, :] % SEG
    phase = 2.0 * math.pi / SEG * turns
    rows = np.concatenate([window * np.cos(phase), -window * np.sin(phase)], axis=0)
    rows = rows.astype(np.float32).astype(jnp.bfloat16)
    return np.repeat(rows, 16, axis=0)


def slope(delta):
    out = np.zeros(delta.shape, np.float32)
    for shift, coefficient in ((1, 8.0), (-1, -8.0), (2, -1.0), (-2, 1.0)):
        out[delta == shift] = coefficient
    return out


def slope_tables():
    lane = np.arange(128)
    along_z = slope(lane[:, None] - lane[None, :])
    edge = np.array([-2, -1, 128, 129])
    edge_rows = slope(edge[:, None] - lane[None, :])
    halo_z = np.zeros((2, 16, 128), np.float32)
    halo_z[0, 0:4] = edge_rows
    halo_z[1, 4:8] = edge_rows
    snap_out = np.repeat(np.arange(8), 32)
    row_out = np.tile(np.arange(32), 8)
    snap_edge = np.repeat(np.arange(8), 2)
    row_edge = np.tile(np.arange(2), 8)
    snap_in = np.concatenate([snap_out, snap_edge, snap_edge])
    row_in = np.concatenate([row_out, row_edge - 2, row_edge + 32])
    snap_sent = np.concatenate([snap_edge, snap_edge])
    row_sent = np.concatenate([row_edge + 30, row_edge])
    sent = snap_sent[:, None] == snap_out[None, :]
    sent = (sent & (row_sent[:, None] == row_out[None, :])).astype(np.float32)
    along_x = slope(row_in[None, :] - row_out[:, None])
    along_x = along_x * (snap_in[None, :] == snap_out[:, None])
    cast = lambda a: a.astype(jnp.bfloat16)
    return cast(along_z), cast(halo_z), cast(along_x), cast(sent)


def kernel(
    vel, offsets, owner, rows_ref, dz_ref, bz_ref, dx_ref, sent_ref, out,
    recv, uext, hz_out, hz_in, h_up, h_down, h_lo, h_hi, om, wm, xs, spec,
    a_buf, c_0, c_1, c_2, c_3, d_buf, e_0, e_1, e_2, e_3, f_buf, g_0, g_1, g_2, g_3, t_buf, out_v,
    own_core, own_1, own_2, tile_1, tile_2,
    a2a_s, a2a_r, hz_s, hz_r, edge_s, edge_r, halo_s, halo_r,
    core_s, core_r, l1_s, l1_r, l2_s, l2_r, g1_s, g1_r, gc_s, gc_r,
    loc_s, out_s,
):
    c_buf, e_buf, g_buf = (c_0, c_1, c_2, c_3), (e_0, e_1, e_2, e_3), (g_0, g_1, g_2, g_3)
    gx, gz, ta = lax.axis_index("gx"), lax.axis_index("gz"), lax.axis_index("ta")
    core = gz % 2
    x = gx % 4
    y = (gz // 2) * 2 + gx // 4

    def chip(px, py, pc):
        return ((py % 2) * 4 + px, (py // 2) * 2 + pc, ta)

    m1 = (1 - core) * x + core * y
    m2 = (1 - core) * y + core * x

    def peer_1(step):
        p = (m1 + step) % 4
        return p, chip((1 - core) * p + core * x, (1 - core) * y + core * p, core)

    def peer_2(step):
        p = (m2 + step) % 4
        return p, chip((1 - core) * x + core * p, (1 - core) * p + core * y, core)

    partner = (gx, (gz // 2) * 2 + 1 - core, ta)
    gx_up, gx_down = ((gx + 1) % 8, gz, ta), ((gx + 7) % 8, gz, ta)
    gz_up, gz_down = (gx, (gz + 1) % 4, ta), (gx, (gz + 3) % 4, ta)

    def remote(src, dst, send, recv_sem, device):
        return pltpu.make_async_remote_copy(
            src_ref=src, dst_ref=dst, send_sem=send, recv_sem=recv_sem,
            device_id=device, device_id_type=MESH,
        )

    everyone = [(gx, gz, (ta + d) % 8) for d in range(1, 8)]
    everyone += [peer_1(d)[1] for d in (1, 2, 3)] + [peer_2(d)[1] for d in (1, 2, 3)]
    everyone += [partner, gx_up, gx_down, gz_up, gz_down]
    barrier = pltpu.get_barrier_semaphore()
    for device in everyone:
        pl.semaphore_signal(barrier, inc=1, device_id=device, device_id_type=MESH)
    pl.semaphore_wait(barrier, len(everyone))

    order = (4, 3, 5, 2, 6, 1, 7)

    def columns(j):
        return pl.ds(pl.multiple_of(j * 128, 128), 128)

    def spread(field, slot):
        copies = []
        for n, d in enumerate(order):
            j = (ta + d) % 8
            copies.append(
                remote(
                    vel.at[field, :, :, columns(j)], recv.at[field, ta],
                    a2a_s.at[slot, n], a2a_r.at[slot, n], (gx, gz, j),
                )
            )
        for copy in copies:
            copy.start()
        mine = pltpu.make_async_copy(
            vel.at[field, :, :, columns(ta)], recv.at[field, ta], loc_s.at[slot]
        )
        mine.start()
        return copies, mine

    edge_up = remote(
        vel.at[U, :, :, 896:1024], uext.at[:, :, 0:128], edge_s.at[0], edge_r.at[0], gz_up
    )
    edge_down = remote(
        vel.at[U, :, :, 0:128], uext.at[:, :, 1152:1280], edge_s.at[1], edge_r.at[1], gz_down
    )
    edge_up.start()
    edge_down.start()
    body = pltpu.make_async_copy(vel.at[U], uext.at[:, :, 128:1152], loc_s.at[3])
    body.start()
    sent_w = spread(W, 0)
    sent_u = spread(U, 1)

    for s in range(NSEG):
        o = owner[s]
        o_gx, o_gz = o // 4, o % 4
        o_x, o_y = o_gx % 4, (o_gz // 2) * 2 + o_gx // 4
        own_core[s] = o_gz % 2
        own_1[s] = (1 - core) * o_x + core * o_y
        own_2[s] = (1 - core) * o_y + core * o_x
    for i in range(PIECE):
        s = jnp.minimum((m1 * PIECE + i) // 14, NSEG - 1)
        tile_1[i] = own_1[s]
        tile_2[i] = own_2[s]

    body.wait()
    edge_up.wait_recv()
    edge_down.wait_recv()
    r_io = lax.broadcasted_iota(jnp.int32, (128, 1280), 0)
    l_io = lax.broadcasted_iota(jnp.int32, (128, 1280), 1)
    r16 = r_io % 16
    r4 = r16 % 4
    target = 128 + 128 * (r_io // 16) + r4 + jnp.where(r4 < 2, -2, 126)
    hit = l_io == target
    packed = jnp.zeros((128, 128), F32)
    for h in range(2):
        select = jnp.where(hit & (r16 // 4 == h), 1.0, 0.0).astype(BF)
        data = uext[4 * h : 4 * h + 4].reshape(128, 1280)
        packed += lax.dot_general(
            select, data, (((1,), (1,)), ((), ())), preferred_element_type=F32
        )
    hz_out[...] = packed.astype(BF).reshape(8, 16, 128)
    sent_hz = []
    for n, d in enumerate(order):
        j = (ta + d) % 8
        sent_hz.append(
            remote(hz_out.at[j], hz_in.at[ta], hz_s.at[n], hz_r.at[n], (gx, gz, j))
        )
    for copy in sent_hz:
        copy.start()
    hz_in[ta] = hz_out[ta]
    sent_v = spread(V, 2)

    col = lax.broadcasted_iota(jnp.int32, (16, 1024), 1)
    lag_io = lax.broadcasted_iota(jnp.int32, (16, 1024), 0)
    same = (
        lax.broadcasted_iota(jnp.int32, (224, 1024), 0) % 16
        == lax.broadcasted_iota(jnp.int32, (224, 1024), 1) % 16
    )

    def build(s, carry):
        one = jnp.where(col // 16 - offsets[s] == lag_io, 1.0, 0.0).astype(BF)
        full = jnp.dot(rows_ref[...], one, preferred_element_type=F32)
        wm[s] = jnp.where(same, full, 0.0).astype(BF)
        return carry

    lax.fori_loop(0, NSEG, build, 0)

    def transform(q, src):
        xs[:, 0:128] = src[:, :, 0:16, :].reshape(1024, 128)
        xs[:, 128:256] = src[:, :, 16:32, :].reshape(1024, 128)
        copies = []
        for s in range(NSEG):
            r = jnp.dot(wm[s], xs[...], preferred_element_type=F32)
            rows = slice(s * 14, s * 14 + 14)
            spec[q, rows] = r.reshape(14, 16, 256)
            lo = r[:, 0:128].astype(BF).reshape(14, 16, 128)
            hi = r[:, 128:256].astype(BF).reshape(14, 16, 128)
            c_buf[q][core, rows] = jnp.where(core == 0, lo, hi)
            a_buf[q, rows] = jnp.where(core == 0, hi, lo)
            copy = remote(
                a_buf.at[q, rows], c_buf[q].at[core, rows],
                core_s.at[q, s], core_r.at[q, s], partner,
            )
            copy.start()
            copies.append(copy)
        return copies

    def scatter(q, before):
        for s, copy in enumerate(before):
            copy.wait_recv()
        for s in range(NSEG):
            d_buf[q, s * 14 : s * 14 + 14] = c_buf[q][own_core[s], s * 14 : s * 14 + 14]
        d_buf[q, J:TILES] = jnp.zeros((2, 16, 128), BF)
        copies = []
        for d in (2, 1, 3):
            p, device = peer_1(d)
            copies.append(
                remote(
                    d_buf.at[q, pl.ds(p * PIECE, PIECE)], e_buf[q].at[m1],
                    l1_s.at[q, d - 1], l1_r.at[q, d - 1], device,
                )
            )
        for copy in copies:
            copy.start()
        e_buf[q][m1] = d_buf[q, pl.ds(m1 * PIECE, PIECE)]
        return copies

    def exchange(q, before):
        for copy in before:
            copy.wait_recv()
        for i in range(PIECE):
            f_buf[q, i] = e_buf[q][tile_1[i], i]
        copies = []
        for d in (2, 1, 3):
            copies.append(
                remote(
                    f_buf.at[q], g_buf[q].at[m2],
                    l2_s.at[q, d - 1], l2_r.at[q, d - 1], peer_2(d)[1],
                )
            )
        for copy in copies:
            copy.start()
        g_buf[q][m2] = f_buf[q]
        return copies

    def piece_of(q, p):
        return t_buf.at[q, core, pl.ds(p * PIECE, PIECE)]

    def gather(q, before):
        for copy in before:
            copy.wait_recv()
        for i in range(PIECE):
            t_buf[q, core, m1 * PIECE + i] = g_buf[q][tile_2[i], i]
        copies = []
        for d in (2, 1, 3):
            copies.append(
                remote(
                    piece_of(q, m1), piece_of(q, m1),
                    g1_s.at[q, d - 1], g1_r.at[q, d - 1], peer_1(d)[1],
                )
            )
        for copy in copies:
            copy.start()
        mine = remote(piece_of(q, m1), piece_of(q, m1), gc_s.at[q, 0], gc_r.at[q, 0], partner)
        mine.start()
        return [mine] + copies

    def share(q, before):
        copies = [before[0]]
        for n, d in ((2, 1), (3, 3), (1, 2)):
            before[n].wait_recv()
            p = (m1 + 4 - d) % 4
            copy = remote(piece_of(q, p), piece_of(q, p), gc_s.at[q, d], gc_r.at[q, d], partner)
            copy.start()
            copies.append(copy)
        forwarded.extend(copies[1:])
        return copies

    scaling = 8.0 / (3.0 * SEG * NSEG)

    def finish(q, before):
        for copy in before:
            copy.wait_recv()

        def one_frequency(k, carry):
            for h in range(2):
                co = jnp.zeros((16, 128), F32)
                quad = jnp.zeros((16, 128), F32)
                for s in range(NSEG):
                    rc = t_buf[q, h, s * 14 + k].astype(F32)
                    rs = t_buf[q, h, s * 14 + F + k].astype(F32)
                    lc = spec[q, s * 14 + k, :, h * 128 : h * 128 + 128]
                    ls = spec[q, s * 14 + F + k, :, h * 128 : h * 128 + 128]
                    co += rc * lc + rs * ls
                    quad += rc * ls - rs * lc
                out_v[q, 0, k, h * 16 : h * 16 + 16, :] = co * scaling
                out_v[q, 1, k, h * 16 : h * 16 + 16, :] = quad * scaling
            return carry

        lax.fori_loop(0, F, one_frequency, 0)
        copy = pltpu.make_async_copy(out_v.at[q], out.at[q], out_s.at[q])
        copy.start()
        return copy

    def vorticity(i, carry):
        u_i = recv[U, i].reshape(256, 128)
        w_i = jnp.concatenate(
            [recv[W, i].reshape(256, 128), h_lo[i], h_hi[i]],
            axis=0,
        )
        across = jnp.dot(dx_ref[...], w_i, preferred_element_type=F32)
        inner = jnp.dot(u_i, dz_ref[...], preferred_element_type=F32)
        outer = jnp.concatenate(
            [
                lax.dot_general(
                    hz_in[i], bz_ref[h], (((0,), (0,)), ((), ())), preferred_element_type=F32
                )
                for h in range(2)
            ],
            axis=0,
        )
        om[i] = ((inner + outer - across) / 12.0).astype(BF).reshape(8, 32, 128)
        return carry

    started = []
    forwarded = []
    chain = {}

    def run(step, q):
        chain[q] = step(q, chain.get(q))
        if step is not share:
            started.extend(chain[q])

    def arrived(sent):
        copies, mine = sent
        mine.wait()
        for copy in copies:
            copy.wait_recv()

    outs = []
    halo = [
        remote(h_up, h_lo, halo_s.at[0], halo_r.at[0], gx_up),
        remote(h_down, h_hi, halo_s.at[1], halo_r.at[1], gx_down),
    ]
    quantity = {"u": U, "v": V, "w": W, "o": OM}
    steps = {"A": scatter, "B": exchange, "G": gather, "H": share}
    sent = {U: sent_u, V: sent_v, W: sent_w}
    for token in ORDER:
        q, step = quantity[token[0]], token[1]
        if step == "T":
            if q == OM:
                for copy in sent_hz + halo:
                    copy.wait_recv()
                lax.fori_loop(0, 8, vorticity, 0)
                chain[q] = om
            else:
                arrived(sent[q])
                if q == W:
                    for i in range(8):
                        edges = jnp.dot(
                            sent_ref[...], recv[W, i].reshape(256, 128), preferred_element_type=F32
                        ).astype(BF)
                        h_up[i] = edges[0:16]
                        h_down[i] = edges[16:32]
                    for copy in halo:
                        copy.start()
                chain[q] = recv.at[q]
            run(transform, q)
        elif step == "F":
            outs.append(finish(q, chain[q]))
        else:
            run(steps[step], q)

    for copies, _ in (sent_w, sent_u, sent_v):
        for copy in copies:
            copy.wait_send()
    for copy in sent_hz + started + forwarded + halo + [edge_up, edge_down]:
        copy.wait_send()
    for copy in outs:
        copy.wait()


def shards(velocity, offsets, owner):
    along_z, halo_z, along_x, edges = slope_tables()
    dma = pltpu.SemaphoreType.DMA
    vmem = lambda *shape: pltpu.VMEM(shape, BF)
    scratch = [
        vmem(3, 8, 8, 32, 128), vmem(8, 32, 1280), vmem(8, 16, 128), vmem(8, 16, 128),
        *[vmem(8, 16, 128)] * 4, vmem(8, 8, 32, 128),
        vmem(NSEG, 224, 1024), vmem(1024, 256), pltpu.VMEM((4, J, 16, 256), F32),
        vmem(4, TILES, 16, 128), *[vmem(2, TILES, 16, 128)] * 4, vmem(4, TILES, 16, 128),
        *[vmem(4, PIECE, 16, 128)] * 4, vmem(4, PIECE, 16, 128), *[vmem(4, PIECE, 16, 128)] * 4,
        vmem(4, 2, TILES, 16, 128),
        pltpu.VMEM((4, 2, F, 32, 128), F32),
        *[pltpu.SMEM((NSEG,), jnp.int32)] * 3, *[pltpu.SMEM((PIECE,), jnp.int32)] * 2,
        dma((3, 7)), dma((3, 7)), dma((7,)), dma((7,)), dma((2,)), dma((2,)), dma((2,)), dma((2,)),
        dma((4, NSEG)), dma((4, NSEG)), dma((4, 3)), dma((4, 3)), dma((4, 3)), dma((4, 3)),
        dma((4, 3)), dma((4, 3)), dma((4, 4)), dma((4, 4)),
        dma((4,)), dma((4,)),
    ]
    return pl.pallas_call(
        kernel,
        out_shape=jax.ShapeDtypeStruct((4, 2, F, 32, 128), F32),
        in_specs=[
            pl.BlockSpec(memory_space=pl.ANY),
            pl.BlockSpec(memory_space=pltpu.SMEM),
            pl.BlockSpec(memory_space=pltpu.SMEM),
        ]
        + [pl.BlockSpec(memory_space=pltpu.VMEM)] * 5,
        out_specs=pl.BlockSpec(memory_space=pl.ANY),
        scratch_shapes=scratch,
        compiler_params=pltpu.CompilerParams(
            collective_id=0, has_side_effects=True, vmem_limit_bytes=56 << 20
        ),
        name="cross_spectra",
    )(
        velocity, offsets, owner, jnp.asarray(table_rows()), jnp.asarray(along_z),
        jnp.asarray(halo_z), jnp.asarray(along_x), jnp.asarray(edges),
    )


def solution(mesh):
    in_specs = (P(None, "ta", "gx", "gz"), P(), P())
    out_specs = P(None, None, None, "gx", ("gz", "ta"))
    return jax.shard_map(shards, mesh=mesh, in_specs=in_specs, out_specs=out_specs, check_vma=False)
```
